32 devices in a mesh: run: 2 (over y), tile: 4 (over z), site: 2 (over x), freq: 2 (over core).
Axes of the slice: x: 2, y: 2, z: 4, core: 2. Of those that a mesh axis runs over, the one named last changes fastest.
Arguments:
- jacobian: bfloat16 [256, 16, 8, 8, 128], P(('run', 'tile', 'site'), None, 'freq'), parts along dimension 0, may hold values from -6 to 6
- footprint: int32 [256, 16], P(('run', 'tile', 'site')), parts along dimension 0, may hold values from 0 to 4095, as said below
- home: int32 [8192], P('run'), parts along dimension 0, may hold values from 0 to 4095, as said below
- residual: float32 [256, 8, 8], P(('run', 'tile', 'site'), 'freq'), parts along dimension 0, may hold values from -6 to 6
- weights: float32 [256], P(('run', 'tile', 'site')), parts along dimension 0, may hold values from 0.2 to 2
- damping: float32 [8192, 128], P(('run', 'tile', 'site')), parts along dimension 0, may hold values from 2 to 50
- step_lengths: float32 [8], replicated, may hold values from 0.2 to 1.2
Outputs:
- model_step: float32 [8192, 128], P(('run', 'tile', 'site')), parts along dimension 0
- change: float32 [256, 8, 8], P(('run', 'tile', 'site'), 'freq'), parts along dimension 0
- curve: float32 [16, 8], P(('run', 'freq')), parts along dimension 0
The draws below stay inside these ranges and needn't reach their ends.
There are 2 independent parts, one for each index of `run`. The reference program is written for one: setup_inputs(seed, part) draws one part's arguments, and reference() takes and returns one part's arrays. A program takes and returns all parts, laid end to end along the dimension named above; an argument that names none is the same for every part. Nothing has to cross between parts.
Inputs may be any that keep to these rules, and one draw needn't show every extreme that they name: home is a permutation of 0 to 4095. `footprint`: of the 256 entries of each aligned block of 16 sites, at most 64 have home[block] // 512 equal to any one value; one value receives exactly 64 entries from every such block.
All inputs are finite; a program needn't handle non-finite values.
Results may differ from the reference program's by a relative error of at most 0.0029.
Values may be sent and summed in bfloat16 or wider, within the bound.
A program may use at most 64 MiB of HBM per device.

```python
import math
import jax
import jax.numpy as jnp
from jax import lax

C = 8
BLK = 128
S_DEV = 16
FOOT = 16
B_DEV = 512
STEPS = 8
OWNERS = 8
CAP = 64
SITES = 128
NB = 4096
FREQ = 8


def routing(key):
    base = jax.random.fold_in(key, 11)
    key_home, key_hot, key_fill, key_mix, key_slot = jax.random.split(base, 5)
    home = jax.random.permutation(key_home, NB).astype(jnp.int32)
    inverse = jnp.argsort(home).astype(jnp.int32)
    entries = S_DEV * FOOT
    hot = jax.random.randint(key_hot, (), 0, OWNERS).astype(jnp.int32)

    def one_source(fill_key, mix_key):
        picks = jax.random.permutation(fill_key, (OWNERS - 1) * CAP)[:entries - CAP] // CAP
        others = jnp.where(picks >= hot, picks + 1, picks).astype(jnp.int32)
        listed = jnp.concatenate([jnp.full((CAP,), hot, jnp.int32), others])
        return jax.random.permutation(mix_key, listed)
    dest = jax.vmap(one_source)(jax.random.split(key_fill, OWNERS), jax.random.split(key_mix, OWNERS))
    slots = jax.random.randint(key_slot, (OWNERS, entries), 0, B_DEV).astype(jnp.int32)
    blocks = inverse[dest * B_DEV + slots]
    return (home, blocks.reshape(SITES, FOOT).astype(jnp.int32))


def draw_footprint(key, part):
    return routing(key)[1]


def draw_home(key, part):
    return routing(key)[0]


def block_scale(own_key, dims, cuts, low, top_value):
    def one(dim, blocks):
        steps = jax.random.uniform(jax.random.fold_in(jax.random.fold_in(own_key, 6), dim), (blocks,), jnp.float32, low / len(cuts), top_value / len(cuts))
        return jnp.repeat(jnp.exp(steps), dims[dim] // blocks).reshape((-1,) + (1,) * (len(dims) - dim - 1))

    loudness = one(*cuts[0])
    for cut in cuts[1:]:
        loudness = loudness * one(*cut)
    return loudness


def gaussian(key, extent, deviation, reach, cuts=(), kind=jnp.bfloat16):
    values = jax.random.normal(key, extent, jnp.float32) * deviation
    if len(cuts) > 0:
        values = block_scale(key, extent, cuts, -0.22, 0.18) * values
    return jnp.clip(values, min=-reach, max=reach).astype(kind)


def setup_inputs(seed: int = 0, part: int = 0) -> dict:
    key_of = jax.random.split(jax.random.key(seed), 8)
    part_keys = jax.random.split(jax.random.fold_in(key_of[7], part), 8)
    jacobian = gaussian(part_keys[0], (SITES, FOOT, FREQ, C, BLK), 1.0, 6.0, ((0, 8), (2, 2)))
    footprint = draw_footprint(jax.random.fold_in(jax.random.fold_in(key_of[7], part), 71), part)
    home = draw_home(jax.random.fold_in(jax.random.fold_in(key_of[7], part), 71), part)
    residual = gaussian(part_keys[3], (SITES, FREQ, C), 1.0, 6.0, ((0, 8), (1, 2)), jnp.float32)
    weights = jnp.clip(jnp.exp(math.log(2.0) - 2.3025851 * jax.random.uniform(part_keys[4], (SITES,), jnp.float32) ** block_scale(part_keys[4], (SITES,), ((0, 8),), -0.2, 0.2)), 0.2, 2.0)
    damping = jnp.clip(jnp.exp(math.log(50.0) - 3.218876 * jax.random.uniform(part_keys[5], (NB, BLK), jnp.float32) ** block_scale(part_keys[5], (NB, BLK), ((0, 8),), -0.2, 0.2)), 2.0, 50.0)
    step_lengths = jnp.clip(jax.random.uniform(key_of[6], (STEPS,), jnp.float32, 0.2, 1.2), 0.2, 1.2)
    return dict(jacobian=jacobian, footprint=footprint, home=home, residual=residual, weights=weights, damping=damping, step_lengths=step_lengths)


def reference(jacobian, footprint, home, residual, weights, damping, step_lengths):
    weighted = (weights[:, None, None] * residual).astype(jnp.bfloat16)
    position = home[footprint]
    jac_groups = jacobian.reshape(OWNERS, S_DEV, FOOT, FREQ, C, BLK)
    wt_groups = weighted.reshape(OWNERS, S_DEV, FREQ, C)
    w_groups = weights.reshape(OWNERS, S_DEV)

    def terms_of(args):
        jac, wtd, wgt = args
        jf = jac.astype(jnp.float32)
        grad = jnp.einsum("skfcb,sfc->skb", jf, wtd.astype(jnp.float32))
        curv = wgt[:, None, None] * jnp.sum(jf * jf, axis=(2, 3))
        return grad, curv

    grad_terms, curve_terms = lax.map(terms_of, (jac_groups, wt_groups, w_groups))
    flat_pos = position.reshape(-1)
    gradient = jax.ops.segment_sum(grad_terms.reshape(-1, BLK), flat_pos, num_segments=NB)
    diagonal = jax.ops.segment_sum(curve_terms.reshape(-1, BLK), flat_pos, num_segments=NB)
    model_step = gradient / (diagonal + damping)
    step_low = model_step.astype(jnp.bfloat16)
    pos_groups = position.reshape(OWNERS, S_DEV, FOOT)

    def change_of(args):
        jac, pos = args
        rows = step_low[pos].astype(jnp.float32)
        return jnp.einsum("skfcb,skb->sfc", jac.astype(jnp.float32), rows)

    change = lax.map(change_of, (jac_groups, pos_groups)).reshape(SITES, FREQ, C)
    gap = residual[:, :, :, None] - step_lengths[None, None, None, :] * change[:, :, :, None]
    curve = jnp.einsum("s,sfca->fa", weights, gap * gap) / (SITES * C)
    return model_step, change, curve
```

```python
import functools

import jax
import jax.numpy as jnp
from jax import lax
from jax.experimental import pallas as pl
from jax.experimental.pallas import tpu as pltpu
from jax.sharding import PartitionSpec as P

MESH = pl.DeviceIdType.MESH
F32, BF16, I32 = jnp.float32, jnp.bfloat16, jnp.int32
LANES = 128
PIECES = 4


def count(shape, dim):
    return lax.broadcasted_iota(I32, shape, dim)


def diagonal(rows, columns):
    return count((rows, columns), 0) == count((rows, columns), 1)


def column_of(row, rows):
    wide = jnp.broadcast_to(row, (rows, row.shape[1]))
    return jnp.sum(jnp.where(diagonal(*wide.shape), wide, 0.0), axis=1, keepdims=True)


def row_of(column, columns):
    wide = jnp.broadcast_to(column, (column.shape[0], columns))
    return jnp.sum(jnp.where(diagonal(*wide.shape), wide, 0.0), axis=0, keepdims=True)


def one_hot(mask):
    return jnp.where(mask, 1.0, 0.0).astype(BF16)


def dot(a, b):
    return jnp.dot(a, b, preferred_element_type=F32)


def kernel(
    sizes,
    jac_any, foot_ref, home_ref, res_ref, w_ref, damp_any, len_ref,
    step_any, change_ref, curve_ref,
    jac, damp, terms, other, split, pick, pick_t, slot_out, slot_in, put, put_t,
    out, inn, both, step, low, rep, ret, entry, curves,
    load_sem, damp_sem, step_sem, pair_sem, total_sem, slot_sem, out_sem, rep_sem, curve_sem,
):
    n, groups, cap, sites, foot, freqs, comps, blocks = sizes
    entries = sites * foot
    rows = n * cap
    run, tile, site, freq = (lax.axis_index(a) for a in ("run", "tile", "site", "freq"))
    me = tile * groups + site
    partner = (run, tile, site, 1 - freq)

    def at(o):
        return (run, o // groups, o % groups, freq)

    def others(body):
        def one(j, carry):
            body((me + j) % n)
            return carry
        lax.fori_loop(1, n, one, 0)

    def place(o):
        return pl.ds(pl.multiple_of(o * cap, cap), cap)

    def remote(src, dst, sems, send, recv, to):
        return pltpu.make_async_remote_copy(
            src_ref=src, dst_ref=dst, send_sem=sems.at[0, send], recv_sem=sems.at[1, recv],
            device_id=to, device_id_type=MESH,
        )

    piece = entries // PIECES
    loads = [
        pltpu.make_async_copy(
            jac_any.at[pl.ds(c * piece, piece)], jac.at[pl.ds(c * piece, piece)], load_sem.at[c]
        )
        for c in range(PIECES)
    ]
    for load in loads:
        load.start()
    damp_load = pltpu.make_async_copy(damp_any, damp, damp_sem)
    damp_load.start()
    barrier = pltpu.get_barrier_semaphore()
    pl.semaphore_signal(barrier, inc=1, device_id=partner, device_id_type=MESH)
    others(
        lambda o: pl.semaphore_signal(barrier, inc=1, device_id=at(o), device_id_type=MESH)
    )

    block = jnp.concatenate(
        [column_of(foot_ref[s : s + 1, :].astype(F32), foot) for s in range(sites)], axis=0
    ).astype(I32)
    home = home_ref[...]
    line = one_hot(count((entries, home.shape[0]), 1) == (block >> 7))
    found = dot(line, (home & 255).astype(F32).astype(BF16)) + 256.0 * dot(
        line, (home >> 8).astype(F32).astype(BF16)
    )
    here = count((entries, LANES), 1) == (block & 127)
    position = jnp.sum(jnp.where(here, found, 0.0), axis=1, keepdims=True)
    wide = -(-n // LANES) * LANES
    owner = count((entries, wide), 1).astype(F32)
    first = owner * float(blocks)
    member = jnp.where((position >= first) & (position < first + float(blocks)), 1.0, 0.0)
    lower = one_hot(count((entries, entries), 0) > count((entries, entries), 1))
    earlier = dot(lower, member.astype(BF16))
    bucket = jnp.sum(member * (earlier + owner * float(cap)), axis=1, keepdims=True)
    slot = position - jnp.sum(member * first, axis=1, keepdims=True)
    pick_t[...] = one_hot(bucket == count((entries, rows), 1).astype(F32))
    pick[...] = one_hot(row_of(bucket, entries) == count((rows, entries), 0).astype(F32))
    lane = count((entries, LANES), 1) - (me * cap) % LANES
    inside = (lane >= 0) & (lane < cap)
    lane = lane.astype(F32)

    def list_slots(o, carry):
        hit = inside & (bucket - (o * cap).astype(F32) == lane)
        slots = jnp.sum(jnp.where(hit, slot, 0.0), axis=0, keepdims=True)
        slot_out[o] = jnp.broadcast_to(slots, (8, LANES))
        return carry

    lax.fori_loop(0, n, list_slots, 0)
    slot_in[me] = slot_out[me]

    pl.semaphore_wait(barrier, n)

    def slot_copy(o, source):
        return remote(slot_out.at[o], slot_in.at[source], slot_sem, o, source, at(o))

    others(lambda o: slot_copy(o, me).start())

    def pair_copy(c):
        span = pl.ds(c * piece, piece)
        return remote(terms.at[1 - freq, span], other.at[span], pair_sem, c, c, partner)

    def site_terms(s, carry):
        w = w_ref[s]
        weighted = jnp.concatenate(
            [
                column_of((res_ref[s, f : f + 1, :] * w).astype(BF16).astype(F32), comps)
                for f in range(freqs)
            ],
            axis=0,
        )
        span = pl.ds(pl.multiple_of(s * foot, foot), foot)
        j = jac[span].astype(F32)
        terms[0, span, :] = jnp.sum(j * weighted[None], axis=1)
        terms[1, span, :] = jnp.sum(j * j, axis=1) * w
        return carry

    for c in range(PIECES):
        loads[c].wait()
        lax.fori_loop(c * sites // PIECES, (c + 1) * sites // PIECES, site_terms, 0)
        pair_copy(c).start()
    for c in range(PIECES):
        span = pl.ds(c * piece, piece)
        pair_copy(c).wait_recv()
        t = terms[freq, span, :] + other[span, :]
        high = t.astype(BF16)
        split[span, :LANES] = high
        split[span, LANES:] = (t - high.astype(F32)).astype(BF16)

    def bucket_rows(o):
        return dot(pick[place(o), :], split[...]).astype(BF16)

    def out_copy(o, source):
        return remote(out.at[o], inn.at[place(source)], out_sem, o, source, at(o))

    def send_out(o):
        out[o] = bucket_rows(o)
        out_copy(o, me).start()

    others(send_out)
    inn[place(me), :] = bucket_rows(me)

    others(lambda o: slot_copy(o, o).wait_recv())
    per = LANES // cap
    for g in range(rows // LANES):
        listed = slot_in[g * per, 0:1, :]
        for p in range(1, per):
            listed = listed + slot_in[g * per + p, 0:1, :]
        span = slice(g * LANES, (g + 1) * LANES)
        put[:, span] = one_hot(listed == count((blocks, LANES), 0).astype(F32))
        put_t[span, :] = one_hot(
            column_of(listed, LANES) == count((LANES, blocks), 1).astype(F32)
        )

    others(lambda o: out_copy(o, o).wait_recv())
    part = blocks // PIECES

    def total_copy(c):
        span = pl.ds(c * part, part)
        return remote(both.at[freq, span], both.at[freq, span], total_sem, c, c, partner)

    for c in range(PIECES):
        t = dot(put[c * part : (c + 1) * part, :], inn[...])
        both[freq, pl.ds(c * part, part), :] = t[:, :LANES] + t[:, LANES:]
        total_copy(c).start()
    damp_load.wait()
    for c in range(PIECES):
        span = pl.ds(c * part, part)
        total_copy(c).wait_recv()
        update = both[0, span, :] / (both[1, span, :] + damp[span, :])
        step[span, :] = update
        low[span, :] = update.astype(BF16)
    step_store = pltpu.make_async_copy(step, step_any, step_sem)
    step_store.start()

    def reply_rows(o):
        return dot(put_t[place(o), :], low[...]).astype(BF16)

    def rep_copy(o, source):
        return remote(rep.at[o], ret.at[place(source)], rep_sem, o, source, at(o))

    def send_reply(o):
        rep[o] = reply_rows(o)
        rep_copy(o, me).start()

    others(send_reply)
    ret[place(me), :] = reply_rows(me)
    others(lambda o: rep_copy(o, o).wait_recv())
    entry[...] = dot(pick_t[...], ret[...])

    steps = len_ref.shape[0]
    eye = diagonal(comps, LANES)

    def site_change(s, sums):
        acc = jnp.zeros((freqs * comps, LANES), F32)
        for k in range(foot):
            e = s * foot + k
            acc = acc + jac[e].astype(F32) * entry[pl.ds(e, 1), :]
        total = jnp.sum(acc, axis=1, keepdims=True)
        ch = jnp.concatenate(
            [
                jnp.sum(
                    jnp.where(eye, total[f * comps : (f + 1) * comps], 0.0), axis=0, keepdims=True
                )
                for f in range(freqs)
            ],
            axis=0,
        )[:, :comps]
        change_ref[s] = ch
        r, w = res_ref[s], w_ref[s]
        gaps = [r - len_ref[a] * ch for a in range(steps)]
        return tuple(t + w * (g * g) for t, g in zip(sums, gaps))

    zero = jnp.zeros((freqs, comps), F32)
    sums = lax.fori_loop(0, sites, site_change, (zero,) * steps)
    mine = jnp.zeros((freqs, LANES), F32)
    for a in range(steps):
        here = count((freqs, LANES), 1) == a
        mine = mine + jnp.where(here, jnp.sum(sums[a], axis=1, keepdims=True), 0.0)
    curves[me] = jnp.zeros((8, LANES), F32)
    curves[me, :freqs, :] = mine

    def curve_copy(o, source):
        return remote(curves.at[me], curves.at[source], curve_sem, o, source, at(o))

    others(lambda o: curve_copy(o, me).start())
    others(lambda o: curve_copy(o, o).wait_recv())
    total = lax.fori_loop(
        0, n, lambda i, t: t + curves[i], jnp.zeros((8, LANES), F32)
    )
    curve_ref[...] = total[:freqs, :steps] * (1.0 / (n * sites * comps))

    for c in range(PIECES):
        pair_copy(c).wait_send()
        total_copy(c).wait_send()
    others(lambda o: slot_copy(o, me).wait_send())
    others(lambda o: out_copy(o, me).wait_send())
    others(lambda o: rep_copy(o, me).wait_send())
    others(lambda o: curve_copy(o, me).wait_send())
    step_store.wait()


def shards(jacobian, footprint, home, residual, weights, damping, step_lengths):
    sites, foot, freqs, comps, width = jacobian.shape
    blocks = damping.shape[0]
    groups = lax.axis_size("site")
    n = lax.axis_size("tile") * groups
    entries = sites * foot
    cap = 16
    while cap < 2 * entries // n:
        cap *= 2
    rows = n * cap
    sizes = (n, groups, cap, sites, foot, freqs, comps, blocks)
    vmem = pl.BlockSpec(memory_space=pltpu.VMEM)
    smem = pl.BlockSpec(memory_space=pltpu.SMEM)
    hbm = pl.BlockSpec(memory_space=pl.ANY)
    dma = pltpu.SemaphoreType.DMA
    return pl.pallas_call(
        functools.partial(kernel, sizes),
        out_shape=(
            jax.ShapeDtypeStruct((blocks, width), F32),
            jax.ShapeDtypeStruct((sites, freqs, comps), F32),
            jax.ShapeDtypeStruct((freqs, step_lengths.shape[0]), F32),
        ),
        in_specs=[hbm, vmem, vmem, vmem, smem, hbm, smem],
        out_specs=(hbm, vmem, vmem),
        scratch_shapes=[
            pltpu.VMEM((entries, freqs * comps, width), BF16),
            pltpu.VMEM((blocks, width), F32),
            pltpu.VMEM((2, entries, width), F32),
            pltpu.VMEM((entries, width), F32),
            pltpu.VMEM((entries, 2 * width), BF16),
            pltpu.VMEM((rows, entries), BF16),
            pltpu.VMEM((entries, rows), BF16),
            pltpu.VMEM((n, 8, LANES), F32),
            pltpu.VMEM((n, 8, LANES), F32),
            pltpu.VMEM((blocks, rows), BF16),
            pltpu.VMEM((rows, blocks), BF16),
            pltpu.VMEM((n, cap, 2 * width), BF16),
            pltpu.VMEM((rows, 2 * width), BF16),
            pltpu.VMEM((2, blocks, width), F32),
            pltpu.VMEM((blocks, width), F32),
            pltpu.VMEM((blocks, width), BF16),
            pltpu.VMEM((n, cap, width), BF16),
            pltpu.VMEM((rows, width), BF16),
            pltpu.VMEM((entries, width), F32),
            pltpu.VMEM((n, 8, LANES), F32),
            dma((PIECES,)),
            dma,
            dma,
            dma((2, PIECES)),
            dma((2, PIECES)),
            dma((2, n)),
            dma((2, n)),
            dma((2, n)),
            dma((2, n)),
        ],
        compiler_params=pltpu.CompilerParams(
            collective_id=0, has_side_effects=True, vmem_limit_bytes=48 * 1024 * 1024
        ),
    )(
        jacobian.reshape(entries, freqs * comps, width),
        footprint,
        home.reshape(-1, LANES),
        residual,
        weights,
        damping,
        step_lengths,
    )


def solution(mesh):
    placed = (
        P(("run", "tile", "site"), None, "freq", None, None),
        P(("run", "tile", "site"), None),
        P("run"),
        P(("run", "tile", "site"), "freq", None),
        P(("run", "tile", "site")),
        P(("run", "tile", "site"), None),
        P(),
    )
    return jax.shard_map(
        shards,
        mesh=mesh,
        in_specs=placed,
        out_specs=(
            P(("run", "tile", "site"), None),
            P(("run", "tile", "site"), "freq", None),
            P(("run", "freq"), None),
        ),
        check_vma=False,
    )
```

```python
import functools

import jax
import jax.numpy as jnp
from jax import lax
from jax.experimental import pallas as pl
from jax.experimental.pallas import tpu as pltpu
from jax.sharding import PartitionSpec as P

MESH = pl.DeviceIdType.MESH
F32, BF16, I32 = jnp.float32, jnp.bfloat16, jnp.int32
LANES = 128
PIECES = 4
VMEM_BYTES = 63 * 1024 * 1024


def count(shape, dim):
    return lax.broadcasted_iota(I32, shape, dim)


def diagonal(rows, columns):
    return count((rows, columns), 0) == count((rows, columns), 1)


def column_of(row, rows):
    wide = jnp.broadcast_to(row, (rows, row.shape[1]))
    return jnp.sum(jnp.where(diagonal(*wide.shape), wide, 0.0), axis=1, keepdims=True)


def row_of(column, columns):
    wide = jnp.broadcast_to(column, (column.shape[0], columns))
    return jnp.sum(jnp.where(diagonal(*wide.shape), wide, 0.0), axis=0, keepdims=True)


def one_hot(mask):
    return jnp.where(mask, 1.0, 0.0).astype(BF16)


def dot(a, b):
    return jnp.dot(a, b, preferred_element_type=F32)


def kernel(
    sizes,
    jac_any, foot_any, home_any, res_any, w_any, damp_any, len_any,
    step_any, change_any, curve_any,
    jac, foot_ref, home_ref, res_ref, w_ref, len_ref, change_ref, curve_ref, damp, terms, other, split, pick, pick_t, slot_out, slot_in, put, put_t,
    out, inn, both, step, low, rep, ret, entry, curves,
    load_sem, small_sem, store_sem, pair_sem, total_sem, slot_sem, out_sem, rep_sem, curve_sem,
):
    n, groups, cap, sites, foot, freqs, comps, blocks = sizes
    entries = sites * foot
    rows = n * cap
    run, tile, site, freq = (lax.axis_index(a) for a in ("run", "tile", "site", "freq"))
    me = tile * groups + site
    partner = (run, tile, site, 1 - freq)

    def at(o):
        return (run, o // groups, o % groups, freq)

    def others(body):
        def one(j, carry):
            body((me + j) % n)
            return carry
        lax.fori_loop(1, n, one, 0, unroll=n <= 16)

    def place(o):
        return pl.ds(pl.multiple_of(o * cap, cap), cap)

    def remote(src, dst, sems, send, recv, to):
        return pltpu.make_async_remote_copy(
            src_ref=src, dst_ref=dst, send_sem=sems.at[0, send], recv_sem=sems.at[1, recv],
            device_id=to, device_id_type=MESH,
        )

    small = [
        pltpu.make_async_copy(source, target, small_sem.at[i])
        for i, (source, target) in enumerate(
            (
                (foot_any, foot_ref),
                (home_any, home_ref),
                (res_any, res_ref),
                (w_any, w_ref),
                (len_any, len_ref),
                (damp_any, damp),
            )
        )
    ]
    for load in small:
        load.start()
    piece = entries // PIECES
    loads = [
        pltpu.make_async_copy(
            jac_any.at[pl.ds(c * piece, piece)], jac.at[pl.ds(c * piece, piece)], load_sem.at[c]
        )
        for c in range(PIECES)
    ]
    for load in loads:
        load.start()
    barrier = pltpu.get_barrier_semaphore()
    pl.semaphore_signal(barrier, inc=1, device_id=partner, device_id_type=MESH)
    others(
        lambda o: pl.semaphore_signal(barrier, inc=1, device_id=at(o), device_id_type=MESH)
    )

    for load in small[:-1]:
        load.wait()


    def pair_copy(c):
        span = pl.ds(c * piece, piece)
        return remote(terms.at[1 - freq, span], other.at[span], pair_sem, c, c, partner)

    site_lane = count((freqs * comps, sites), 1)
    w_row = w_ref[...]
    residual = res_ref[...].reshape(freqs * comps, sites)
    weighted = (residual * w_row).astype(BF16).astype(F32)

    def site_terms(s, carry):
        col = jnp.sum(jnp.where(site_lane == s, weighted, 0.0), axis=1, keepdims=True)
        w = jnp.sum(jnp.where(site_lane[:1] == s, w_row, 0.0), axis=1, keepdims=True)
        span = pl.ds(pl.multiple_of(s * foot, foot), foot)
        j = jac[span].astype(F32)
        terms[0, span, :] = jnp.sum(j * col[None], axis=1)
        terms[1, span, :] = jnp.sum(j * j, axis=1) * w
        return carry

    for c in range(PIECES):
        loads[c].wait()
        lax.fori_loop(c * sites // PIECES, (c + 1) * sites // PIECES, site_terms, 0, unroll=2)
        if c == 0:
            pl.semaphore_wait(barrier, n)
        pair_copy(c).start()

    block = jnp.concatenate(
        [column_of(foot_ref[s : s + 1, :].astype(F32), foot) for s in range(sites)], axis=0
    ).astype(I32)
    home = home_ref[...]
    line = one_hot(count((entries, home.shape[0]), 1) == (block >> 7))
    found = dot(line, (home & 255).astype(F32).astype(BF16)) + 256.0 * dot(
        line, (home >> 8).astype(F32).astype(BF16)
    )
    here = count((entries, LANES), 1) == (block & 127)
    position = jnp.sum(jnp.where(here, found, 0.0), axis=1, keepdims=True)
    wide = -(-n // LANES) * LANES
    owner = count((entries, wide), 1).astype(F32)
    first = owner * float(blocks)
    member = jnp.where((position >= first) & (position < first + float(blocks)), 1.0, 0.0)
    lower = one_hot(count((entries, entries), 0) > count((entries, entries), 1))
    earlier = dot(lower, member.astype(BF16))
    bucket = jnp.sum(member * (earlier + owner * float(cap)), axis=1, keepdims=True)
    slot = position - jnp.sum(member * first, axis=1, keepdims=True)
    pick_t[...] = one_hot(bucket == count((entries, rows), 1).astype(F32))
    pick[...] = one_hot(row_of(bucket, entries) == count((rows, entries), 0).astype(F32))
    lane = count((entries, LANES), 1) - (me * cap) % LANES
    inside = (lane >= 0) & (lane < cap)
    lane = lane.astype(F32)

    def list_slots(o, carry):
        hit = inside & (bucket - (o * cap).astype(F32) == lane)
        slots = jnp.sum(jnp.where(hit, slot, 0.0), axis=0, keepdims=True)
        slot_out[o] = jnp.broadcast_to(slots, (8, LANES))
        return carry

    lax.fori_loop(0, n, list_slots, 0)
    slot_in[me] = slot_out[me]

    def slot_copy(o, source):
        return remote(slot_out.at[o], slot_in.at[source], slot_sem, o, source, at(o))

    others(lambda o: slot_copy(o, me).start())
    for c in range(PIECES):
        span = pl.ds(c * piece, piece)
        pair_copy(c).wait_recv()
        t = terms[freq, span, :] + other[span, :]
        high = t.astype(BF16)
        split[span, :LANES] = high
        split[span, LANES:] = (t - high.astype(F32)).astype(BF16)

    out[...] = dot(pick[...], split[...]).astype(BF16)

    def out_copy(o, source):
        return remote(out.at[place(o)], inn.at[place(source)], out_sem, o, source, at(o))

    others(lambda o: out_copy(o, me).start())
    inn[place(me), :] = out[place(me), :]

    others(lambda o: slot_copy(o, o).wait_recv())
    per = LANES // cap
    for g in range(rows // LANES):
        listed = slot_in[g * per, 0:1, :]
        for p in range(1, per):
            listed = listed + slot_in[g * per + p, 0:1, :]
        span = slice(g * LANES, (g + 1) * LANES)
        put[:, span] = one_hot(listed == count((blocks, LANES), 0).astype(F32))
        put_t[span, :] = one_hot(
            column_of(listed, LANES) == count((LANES, blocks), 1).astype(F32)
        )

    others(lambda o: out_copy(o, o).wait_recv())
    part = blocks // PIECES

    def total_copy(c):
        span = pl.ds(c * part, part)
        return remote(both.at[freq, span], both.at[freq, span], total_sem, c, c, partner)

    for c in range(PIECES):
        t = dot(put[c * part : (c + 1) * part, :], inn[...])
        both[freq, pl.ds(c * part, part), :] = t[:, :LANES] + t[:, LANES:]
        total_copy(c).start()
    small[-1].wait()
    for c in range(PIECES):
        span = pl.ds(c * part, part)
        total_copy(c).wait_recv()
        update = both[0, span, :] / (both[1, span, :] + damp[span, :])
        step[span, :] = update
        low[span, :] = update.astype(BF16)
    step_store = pltpu.make_async_copy(step, step_any, store_sem.at[0])
    step_store.start()

    rep[...] = dot(put_t[...], low[...]).astype(BF16)

    def rep_copy(o, source):
        return remote(rep.at[place(o)], ret.at[place(source)], rep_sem, o, source, at(o))

    others(lambda o: rep_copy(o, me).start())
    ret[place(me), :] = rep[place(me), :]
    others(lambda o: rep_copy(o, o).wait_recv())
    entry[...] = dot(pick_t[...], ret[...])

    steps = len_ref.shape[1]

    def site_change(s, change):
        acc = jnp.zeros((freqs * comps, LANES), F32)
        for k in range(foot):
            e = s * foot + k
            acc = acc + jac[e].astype(F32) * entry[pl.ds(e, 1), :]
        total = jnp.sum(acc, axis=1, keepdims=True)
        return jnp.where(site_lane == s, total, change)

    change = lax.fori_loop(0, sites, site_change, jnp.zeros((freqs * comps, sites), F32), unroll=4)
    change_ref[...] = change.reshape(freqs, comps, sites)
    change_store = pltpu.make_async_copy(change_ref, change_any, store_sem.at[1])
    change_store.start()
    mine = jnp.zeros((freqs, LANES), F32)
    for a in range(steps):
        gap = residual - len_ref[0:1, a : a + 1] * change
        lost = (w_row * (gap * gap)).reshape(freqs, comps, sites)
        lost = jnp.sum(jnp.sum(lost, axis=1), axis=1, keepdims=True)
        mine = mine + jnp.where(count((freqs, LANES), 1) == a, lost, 0.0)
    curves[me] = jnp.zeros((8, LANES), F32)
    curves[me, :freqs, :] = mine

    def curve_copy(o, source):
        return remote(curves.at[me], curves.at[source], curve_sem, o, source, at(o))

    others(lambda o: curve_copy(o, me).start())
    others(lambda o: curve_copy(o, o).wait_recv())
    total = lax.fori_loop(
        0, n, lambda i, t: t + curves[i], jnp.zeros((8, LANES), F32)
    )
    curve_ref[...] = total[:freqs, :steps] * (1.0 / (n * sites * comps))

    curve_store = pltpu.make_async_copy(curve_ref, curve_any, store_sem.at[2])
    curve_store.start()
    for c in range(PIECES):
        pair_copy(c).wait_send()
        total_copy(c).wait_send()
    others(lambda o: slot_copy(o, me).wait_send())
    others(lambda o: out_copy(o, me).wait_send())
    others(lambda o: rep_copy(o, me).wait_send())
    others(lambda o: curve_copy(o, me).wait_send())
    step_store.wait()
    change_store.wait()
    curve_store.wait()


def shards(jacobian, footprint, home, residual, weights, damping, step_lengths):
    sites, foot, freqs, comps, width = jacobian.shape
    blocks = damping.shape[0]
    groups = lax.axis_size("site")
    n = lax.axis_size("tile") * groups
    entries = sites * foot
    cap = 16
    while cap < 2 * entries // n:
        cap *= 2
    rows = n * cap
    sizes = (n, groups, cap, sites, foot, freqs, comps, blocks)
    hbm = pl.BlockSpec(memory_space=pl.ANY)
    dma = pltpu.SemaphoreType.DMA
    model_step, change, curve = pl.pallas_call(
        functools.partial(kernel, sizes),
        out_shape=(
            jax.ShapeDtypeStruct((blocks, width), F32),
            jax.ShapeDtypeStruct((freqs, comps, sites), F32),
            jax.ShapeDtypeStruct((freqs, step_lengths.shape[0]), F32),
        ),
        in_specs=[hbm] * 7,
        out_specs=(hbm,) * 3,
        scratch_shapes=[
            pltpu.VMEM((entries, freqs * comps, width), BF16),
            pltpu.VMEM((sites, foot), I32),
            pltpu.VMEM((home.shape[0] // LANES, LANES), I32),
            pltpu.VMEM((freqs, comps, sites), F32),
            pltpu.VMEM((1, sites), F32),
            pltpu.VMEM((1, step_lengths.shape[0]), F32),
            pltpu.VMEM((freqs, comps, sites), F32),
            pltpu.VMEM((freqs, step_lengths.shape[0]), F32),
            pltpu.VMEM((blocks, width), F32),
            pltpu.VMEM((2, entries, width), F32),
            pltpu.VMEM((entries, width), F32),
            pltpu.VMEM((entries, 2 * width), BF16),
            pltpu.VMEM((rows, entries), BF16),
            pltpu.VMEM((entries, rows), BF16),
            pltpu.VMEM((n, 8, LANES), F32),
            pltpu.VMEM((n, 8, LANES), F32),
            pltpu.VMEM((blocks, rows), BF16),
            pltpu.VMEM((rows, blocks), BF16),
            pltpu.VMEM((rows, 2 * width), BF16),
            pltpu.VMEM((rows, 2 * width), BF16),
            pltpu.VMEM((2, blocks, width), F32),
            pltpu.VMEM((blocks, width), F32),
            pltpu.VMEM((blocks, width), BF16),
            pltpu.VMEM((rows, width), BF16),
            pltpu.VMEM((rows, width), BF16),
            pltpu.VMEM((entries, width), F32),
            pltpu.VMEM((n, 8, LANES), F32),
            dma((PIECES,)),
            dma((6,)),
            dma((3,)),
            dma((2, PIECES)),
            dma((2, PIECES)),
            dma((2, n)),
            dma((2, n)),
            dma((2, n)),
            dma((2, n)),
        ],
        compiler_params=pltpu.CompilerParams(
            collective_id=0, has_side_effects=True, vmem_limit_bytes=VMEM_BYTES
        ),
    )(
        jacobian.reshape(entries, freqs * comps, width),
        footprint,
        home.reshape(-1, LANES),
        residual.transpose(1, 2, 0),
        weights.reshape(1, -1),
        damping,
        step_lengths.reshape(1, -1),
    )
    return model_step, change.transpose(2, 0, 1), curve


def solution(mesh):
    placed = (
        P(("run", "tile", "site"), None, "freq", None, None),
        P(("run", "tile", "site"), None),
        P("run"),
        P(("run", "tile", "site"), "freq", None),
        P(("run", "tile", "site")),
        P(("run", "tile", "site"), None),
        P(),
    )
    return jax.shard_map(
        shards,
        mesh=mesh,
        in_specs=placed,
        out_specs=(
            P(("run", "tile", "site"), None),
            P(("run", "tile", "site"), "freq", None),
            P(("run", "freq"), None),
        ),
        check_vma=False,
    )
```

```python
import functools

import jax
import jax.numpy as jnp
from jax import lax
from jax.experimental import pallas as pl
from jax.experimental.pallas import tpu as pltpu
from jax.sharding import PartitionSpec as P

MESH = pl.DeviceIdType.MESH
F32, BF16, I32 = jnp.float32, jnp.bfloat16, jnp.int32
LANES = 128
PIECES = 4
VMEM_BYTES = 32 * 1024 * 1024


def count(shape, dim):
    return lax.broadcasted_iota(I32, shape, dim)


def diagonal(rows, columns):
    return count((rows, columns), 0) == count((rows, columns), 1)


def column_of(row, rows):
    wide = jnp.broadcast_to(row, (rows, row.shape[1]))
    return jnp.sum(jnp.where(diagonal(*wide.shape), wide, 0.0), axis=1, keepdims=True)


def row_of(column, columns):
    wide = jnp.broadcast_to(column, (column.shape[0], columns))
    return jnp.sum(jnp.where(diagonal(*wide.shape), wide, 0.0), axis=0, keepdims=True)


def one_hot(mask):
    return jnp.where(mask, 1.0, 0.0).astype(BF16)


def dot(a, b):
    return jnp.dot(a, b, preferred_element_type=F32)


def kernel(
    sizes,
    jac_any, foot_any, home_any, res_any, w_any, damp_any, len_any,
    step, change_ref, curve_ref,
    jac, foot_ref, home_ref, res_ref, w_ref, len_ref, damp, terms, other, split, pick, pick_t, slot_out, slot_in, put, put_t,
    out, inn, both, low, rep, ret, entry, curves,
    load_sem, small_sem, pair_sem, total_sem, slot_sem, out_sem, rep_sem, curve_sem,
):
    n, groups, cap, sites, foot, freqs, comps, blocks = sizes
    entries = sites * foot
    rows = n * cap
    run, tile, site, freq = (lax.axis_index(a) for a in ("run", "tile", "site", "freq"))
    me = tile * groups + site
    partner = (run, tile, site, 1 - freq)

    def at(o):
        return (run, o // groups, o % groups, freq)

    def others(body):
        def one(j, carry):
            body((me + j) % n)
            return carry
        lax.fori_loop(1, n, one, 0, unroll=n <= 16)

    def place(o):
        return pl.ds(pl.multiple_of(o * cap, cap), cap)

    def remote(src, dst, sems, send, recv, to):
        return pltpu.make_async_remote_copy(
            src_ref=src, dst_ref=dst, send_sem=sems.at[0, send], recv_sem=sems.at[1, recv],
            device_id=to, device_id_type=MESH,
        )

    small = [
        pltpu.make_async_copy(source, target, small_sem.at[i])
        for i, (source, target) in enumerate(
            (
                (foot_any, foot_ref),
                (home_any, home_ref),
                (res_any, res_ref),
                (w_any, w_ref),
                (len_any, len_ref),
                (damp_any, damp),
            )
        )
    ]
    for load in small:
        load.start()
    piece = entries // PIECES
    loads = [
        pltpu.make_async_copy(
            jac_any.at[pl.ds(c * piece, piece)], jac.at[pl.ds(c * piece, piece)], load_sem.at[c]
        )
        for c in range(PIECES)
    ]
    for load in loads:
        load.start()
    barrier = pltpu.get_barrier_semaphore()
    pl.semaphore_signal(barrier, inc=1, device_id=partner, device_id_type=MESH)
    others(
        lambda o: pl.semaphore_signal(barrier, inc=1, device_id=at(o), device_id_type=MESH)
    )

    for load in small[:-1]:
        load.wait()


    def pair_copy(c):
        span = pl.ds(c * piece, piece)
        return remote(terms.at[1 - freq, span], other.at[span], pair_sem, c, c, partner)

    site_lane = count((freqs * comps, sites), 1)
    w_row = w_ref[...]
    residual = res_ref[...].reshape(freqs * comps, sites)
    weighted = (residual * w_row).astype(BF16).astype(F32)

    def site_terms(s, carry):
        col = jnp.sum(jnp.where(site_lane == s, weighted, 0.0), axis=1, keepdims=True)
        w = jnp.sum(jnp.where(site_lane[:1] == s, w_row, 0.0), axis=1, keepdims=True)
        span = pl.ds(pl.multiple_of(s * foot, foot), foot)
        j = jac[span].astype(F32)
        terms[0, span, :] = jnp.sum(j * col[None], axis=1)
        terms[1, span, :] = jnp.sum(j * j, axis=1) * w
        return carry

    for c in range(PIECES):
        loads[c].wait()
        lax.fori_loop(c * sites // PIECES, (c + 1) * sites // PIECES, site_terms, 0, unroll=2)

    block = jnp.concatenate(
        [column_of(foot_ref[s : s + 1, :].astype(F32), foot) for s in range(sites)], axis=0
    ).astype(I32)
    home = home_ref[...]
    line = one_hot(count((entries, home.shape[0]), 1) == (block >> 7))
    found = dot(line, (home & 255).astype(F32).astype(BF16)) + 256.0 * dot(
        line, (home >> 8).astype(F32).astype(BF16)
    )
    here = count((entries, LANES), 1) == (block & 127)
    position = jnp.sum(jnp.where(here, found, 0.0), axis=1, keepdims=True)
    wide = -(-n // LANES) * LANES
    owner = count((entries, wide), 1).astype(F32)
    first = owner * float(blocks)
    member = jnp.where((position >= first) & (position < first + float(blocks)), 1.0, 0.0)
    lower = one_hot(count((entries, entries), 0) > count((entries, entries), 1))
    earlier = dot(lower, member.astype(BF16))
    bucket = jnp.sum(member * (earlier + owner * float(cap)), axis=1, keepdims=True)
    slot = position - jnp.sum(member * first, axis=1, keepdims=True)
    pick_t[...] = one_hot(bucket == count((entries, rows), 1).astype(F32))
    pick[...] = one_hot(row_of(bucket, entries) == count((rows, entries), 0).astype(F32))
    lane = count((entries, LANES), 1) - (me * cap) % LANES
    inside = (lane >= 0) & (lane < cap)
    lane = lane.astype(F32)

    def list_slots(o, carry):
        hit = inside & (bucket - (o * cap).astype(F32) == lane)
        slots = jnp.sum(jnp.where(hit, slot, 0.0), axis=0, keepdims=True)
        slot_out[o] = jnp.broadcast_to(slots, (8, LANES))
        return carry

    lax.fori_loop(0, n, list_slots, 0)
    slot_in[me] = slot_out[me]

    pl.semaphore_wait(barrier, n)
    for c in range(PIECES):
        pair_copy(c).start()

    def slot_copy(o, source):
        return remote(slot_out.at[o], slot_in.at[source], slot_sem, o, source, at(o))

    others(lambda o: slot_copy(o, me).start())
    for c in range(PIECES):
        span = pl.ds(c * piece, piece)
        pair_copy(c).wait_recv()
        t = terms[freq, span, :] + other[span, :]
        high = t.astype(BF16)
        split[span, :LANES] = high
        split[span, LANES:] = (t - high.astype(F32)).astype(BF16)

    out[...] = dot(pick[...], split[...]).astype(BF16)

    def out_copy(o, source):
        return remote(out.at[place(o)], inn.at[place(source)], out_sem, o, source, at(o))

    others(lambda o: out_copy(o, me).start())
    inn[place(me), :] = out[place(me), :]

    others(lambda o: slot_copy(o, o).wait_recv())
    per = LANES // cap
    for g in range(rows // LANES):
        listed = slot_in[g * per, 0:1, :]
        for p in range(1, per):
            listed = listed + slot_in[g * per + p, 0:1, :]
        span = slice(g * LANES, (g + 1) * LANES)
        put[:, span] = one_hot(listed == count((blocks, LANES), 0).astype(F32))
        put_t[span, :] = one_hot(
            column_of(listed, LANES) == count((LANES, blocks), 1).astype(F32)
        )

    others(lambda o: out_copy(o, o).wait_recv())
    part = blocks // PIECES

    def total_copy(c):
        span = pl.ds(c * part, part)
        return remote(both.at[freq, span], both.at[freq, span], total_sem, c, c, partner)

    for c in range(PIECES):
        t = dot(put[c * part : (c + 1) * part, :], inn[...])
        both[freq, pl.ds(c * part, part), :] = t[:, :LANES] + t[:, LANES:]
        total_copy(c).start()
    small[-1].wait()
    for c in range(PIECES):
        span = pl.ds(c * part, part)
        total_copy(c).wait_recv()
        update = both[0, span, :] / (both[1, span, :] + damp[span, :])
        step[span, :] = update
        low[span, :] = update.astype(BF16)

    rep[...] = dot(put_t[...], low[...]).astype(BF16)

    def rep_copy(o, source):
        return remote(rep.at[place(o)], ret.at[place(source)], rep_sem, o, source, at(o))

    others(lambda o: rep_copy(o, me).start())
    ret[place(me), :] = rep[place(me), :]
    others(lambda o: rep_copy(o, o).wait_recv())
    entry[...] = dot(pick_t[...], ret[...])

    steps = len_ref.shape[1]

    def site_change(s, change):
        acc = jnp.zeros((freqs * comps, LANES), F32)
        for k in range(foot):
            e = s * foot + k
            acc = acc + jac[e].astype(F32) * entry[pl.ds(e, 1), :]
        total = jnp.sum(acc, axis=1, keepdims=True)
        return jnp.where(site_lane == s, total, change)

    change = lax.fori_loop(0, sites, site_change, jnp.zeros((freqs * comps, sites), F32), unroll=4)
    change_ref[...] = change.reshape(freqs, comps, sites)
    mine = jnp.zeros((freqs, LANES), F32)
    for a in range(steps):
        gap = residual - len_ref[0:1, a : a + 1] * change
        lost = (w_row * (gap * gap)).reshape(freqs, comps, sites)
        lost = jnp.sum(jnp.sum(lost, axis=1), axis=1, keepdims=True)
        mine = mine + jnp.where(count((freqs, LANES), 1) == a, lost, 0.0)
    curves[me] = jnp.zeros((8, LANES), F32)
    curves[me, :freqs, :] = mine

    def curve_copy(o, source):
        return remote(curves.at[me], curves.at[source], curve_sem, o, source, at(o))

    others(lambda o: curve_copy(o, me).start())
    others(lambda o: curve_copy(o, o).wait_recv())
    total = lax.fori_loop(
        0, n, lambda i, t: t + curves[i], jnp.zeros((8, LANES), F32)
    )
    curve_ref[...] = total[:freqs, :steps] * (1.0 / (n * sites * comps))

    for c in range(PIECES):
        pair_copy(c).wait_send()
        total_copy(c).wait_send()
    others(lambda o: slot_copy(o, me).wait_send())
    others(lambda o: out_copy(o, me).wait_send())
    others(lambda o: rep_copy(o, me).wait_send())
    others(lambda o: curve_copy(o, me).wait_send())


def store(*refs):
    count = len(refs) // 2
    sems = refs[-1]
    copies = [
        pltpu.make_async_copy(refs[i], refs[count + i], sems.at[i]) for i in range(count)
    ]
    for copy in copies:
        copy.start()
    for copy in copies:
        copy.wait()


def shards(jacobian, footprint, home, residual, weights, damping, step_lengths):
    sites, foot, freqs, comps, width = jacobian.shape
    blocks = damping.shape[0]
    groups = lax.axis_size("site")
    n = lax.axis_size("tile") * groups
    entries = sites * foot
    cap = 16
    while cap < 2 * entries // n:
        cap *= 2
    rows = n * cap
    sizes = (n, groups, cap, sites, foot, freqs, comps, blocks)
    hbm = pl.BlockSpec(memory_space=pltpu.HBM)
    free = pl.BlockSpec(memory_space=pl.ANY)
    vmem = pl.BlockSpec(memory_space=pltpu.VMEM)
    dma = pltpu.SemaphoreType.DMA
    results = pl.pallas_call(
        functools.partial(kernel, sizes),
        out_shape=(
            jax.ShapeDtypeStruct((blocks, width), F32),
            jax.ShapeDtypeStruct((freqs, comps, sites), F32),
            jax.ShapeDtypeStruct((freqs, step_lengths.shape[0]), F32),
        ),
        in_specs=[hbm] * 7,
        out_specs=(vmem,) * 3,
        scratch_shapes=[
            pltpu.VMEM((entries, freqs * comps, width), BF16),
            pltpu.VMEM((sites, foot), I32),
            pltpu.VMEM((home.shape[0] // LANES, LANES), I32),
            pltpu.VMEM((freqs, comps, sites), F32),
            pltpu.VMEM((1, sites), F32),
            pltpu.VMEM((1, step_lengths.shape[0]), F32),
            pltpu.VMEM((blocks, width), F32),
            pltpu.VMEM((2, entries, width), F32),
            pltpu.VMEM((entries, width), F32),
            pltpu.VMEM((entries, 2 * width), BF16),
            pltpu.VMEM((rows, entries), BF16),
            pltpu.VMEM((entries, rows), BF16),
            pltpu.VMEM((n, 8, LANES), F32),
            pltpu.VMEM((n, 8, LANES), F32),
            pltpu.VMEM((blocks, rows), BF16),
            pltpu.VMEM((rows, blocks), BF16),
            pltpu.VMEM((rows, 2 * width), BF16),
            pltpu.VMEM((rows, 2 * width), BF16),
            pltpu.VMEM((2, blocks, width), F32),
            pltpu.VMEM((blocks, width), BF16),
            pltpu.VMEM((rows, width), BF16),
            pltpu.VMEM((rows, width), BF16),
            pltpu.VMEM((entries, width), F32),
            pltpu.VMEM((n, 8, LANES), F32),
            dma((PIECES,)),
            dma((6,)),
            dma((2, PIECES)),
            dma((2, PIECES)),
            dma((2, n)),
            dma((2, n)),
            dma((2, n)),
            dma((2, n)),
        ],
        compiler_params=pltpu.CompilerParams(
            collective_id=0, has_side_effects=True, vmem_limit_bytes=VMEM_BYTES
        ),
    )(
        *(
            pltpu.with_memory_space_constraint(x, pltpu.HBM)
            for x in (
                jacobian.reshape(entries, freqs * comps, width),
                footprint,
                home.reshape(-1, LANES),
                residual.transpose(1, 2, 0),
                weights.reshape(1, -1),
                damping,
                step_lengths.reshape(1, -1),
            )
        )
    )
    model_step, change, curve = pl.pallas_call(
        store,
        out_shape=tuple(jax.ShapeDtypeStruct(r.shape, r.dtype) for r in results),
        in_specs=[free] * len(results),
        out_specs=(hbm,) * len(results),
        scratch_shapes=[dma((len(results),))],
        compiler_params=pltpu.CompilerParams(vmem_limit_bytes=VMEM_BYTES // 8),
    )(*results)
    return model_step, change.transpose(2, 0, 1), curve


def solution(mesh):
    placed = (
        P(("run", "tile", "site"), None, "freq", None, None),
        P(("run", "tile", "site"), None),
        P("run"),
        P(("run", "tile", "site"), "freq", None),
        P(("run", "tile", "site")),
        P(("run", "tile", "site"), None),
        P(),
    )
    return jax.shard_map(
        shards,
        mesh=mesh,
        in_specs=placed,
        out_specs=(
            P(("run", "tile", "site"), None),
            P(("run", "tile", "site"), "freq", None),
            P(("run", "freq"), None),
        ),
        check_vma=False,
    )
```

```python
import functools

import jax
import jax.numpy as jnp
from jax import lax
from jax.experimental import pallas as pl
from jax.experimental.pallas import tpu as pltpu
from jax.sharding import PartitionSpec as P

MESH = pl.DeviceIdType.MESH
F32, BF16, I32 = jnp.float32, jnp.bfloat16, jnp.int32
LANES = 128
PIECES = 4
VMEM_BYTES = 32 * 1024 * 1024


def count(shape, dim):
    return lax.broadcasted_iota(I32, shape, dim)


def diagonal(rows, columns):
    return count((rows, columns), 0) == count((rows, columns), 1)


def column_of(row, rows):
    wide = jnp.broadcast_to(row, (rows, row.shape[1]))
    return jnp.sum(jnp.where(diagonal(*wide.shape), wide, 0.0), axis=1, keepdims=True)


def row_of(column, columns):
    wide = jnp.broadcast_to(column, (column.shape[0], columns))
    return jnp.sum(jnp.where(diagonal(*wide.shape), wide, 0.0), axis=0, keepdims=True)


def one_hot(mask):
    return jnp.where(mask, 1.0, 0.0).astype(BF16)


def dot(a, b):
    return jnp.dot(a, b, preferred_element_type=F32)


def kernel(
    sizes,
    jac_any, foot_any, home_any, res_any, w_any, damp_any, len_any,
    step, change_ref, curve_ref,
    jac, foot_ref, home_ref, res_ref, w_ref, len_ref, damp, terms, other, split, pick, pick_t, slot_out, slot_in, put, put_t,
    out, inn, both, low, rep, ret, entry, curves,
    load_sem, small_sem, pair_sem, total_sem, slot_sem, out_sem, rep_sem, curve_sem,
):
    n, groups, cap, sites, foot, freqs, comps, blocks = sizes
    entries = sites * foot
    rows = n * cap
    run, tile, site, freq = (lax.axis_index(a) for a in ("run", "tile", "site", "freq"))
    me = tile * groups + site
    partner = (run, tile, site, 1 - freq)

    def at(o):
        return (run, o // groups, o % groups, freq)

    def others(body):
        def one(j, carry):
            body((me + j) % n)
            return carry
        if n > 16:
            lax.fori_loop(1, n, one, 0)
        else:
            for j in sorted(range(1, n), key=lambda j: abs(2 * j - n)):
                one(j, 0)

    def place(o):
        return pl.ds(pl.multiple_of(o * cap, cap), cap)

    def remote(src, dst, sems, send, recv, to):
        return pltpu.make_async_remote_copy(
            src_ref=src, dst_ref=dst, send_sem=sems.at[0, send], recv_sem=sems.at[1, recv],
            device_id=to, device_id_type=MESH,
        )

    small = [
        pltpu.make_async_copy(source, target, small_sem.at[i])
        for i, (source, target) in enumerate(
            (
                (foot_any, foot_ref),
                (home_any, home_ref),
                (res_any, res_ref),
                (w_any, w_ref),
                (len_any, len_ref),
                (damp_any, damp),
            )
        )
    ]
    for load in small:
        load.start()
    piece = entries // PIECES
    loads = [
        pltpu.make_async_copy(
            jac_any.at[pl.ds(c * piece, piece)], jac.at[pl.ds(c * piece, piece)], load_sem.at[c]
        )
        for c in range(PIECES)
    ]
    for load in loads:
        load.start()
    barrier = pltpu.get_barrier_semaphore()
    pl.semaphore_signal(barrier, inc=1, device_id=partner, device_id_type=MESH)
    others(
        lambda o: pl.semaphore_signal(barrier, inc=1, device_id=at(o), device_id_type=MESH)
    )

    for load in small[:-1]:
        load.wait()


    def pair_copy(c):
        span = pl.ds(c * piece, piece)
        return remote(terms.at[1 - freq, span], other.at[span], pair_sem, c, c, partner)

    site_lane = count((freqs * comps, sites), 1)
    w_row = w_ref[...]
    residual = res_ref[...].reshape(freqs * comps, sites)
    weighted = (residual * w_row).astype(BF16).astype(F32)

    def site_terms(s, carry):
        col = jnp.sum(jnp.where(site_lane == s, weighted, 0.0), axis=1, keepdims=True)
        w = jnp.sum(jnp.where(site_lane[:1] == s, w_row, 0.0), axis=1, keepdims=True)
        span = pl.ds(pl.multiple_of(s * foot, foot), foot)
        j = jac[span].astype(F32)
        terms[0, span, :] = jnp.sum(j * col[None], axis=1)
        terms[1, span, :] = jnp.sum(j * j, axis=1) * w
        return carry

    for c in range(PIECES):
        loads[c].wait()
        lax.fori_loop(c * sites // PIECES, (c + 1) * sites // PIECES, site_terms, 0, unroll=2)

    block = jnp.concatenate(
        [column_of(foot_ref[s : s + 1, :].astype(F32), foot) for s in range(sites)], axis=0
    ).astype(I32)
    home = home_ref[...]
    line = one_hot(count((entries, home.shape[0]), 1) == (block >> 7))
    found = dot(line, (home & 255).astype(F32).astype(BF16)) + 256.0 * dot(
        line, (home >> 8).astype(F32).astype(BF16)
    )
    here = count((entries, LANES), 1) == (block & 127)
    position = jnp.sum(jnp.where(here, found, 0.0), axis=1, keepdims=True)
    wide = -(-n // LANES) * LANES
    owner = count((entries, wide), 1).astype(F32)
    first = owner * float(blocks)
    member = jnp.where((position >= first) & (position < first + float(blocks)), 1.0, 0.0)
    lower = one_hot(count((entries, entries), 0) > count((entries, entries), 1))
    earlier = dot(lower, member.astype(BF16))
    bucket = jnp.sum(member * (earlier + owner * float(cap)), axis=1, keepdims=True)
    slot = position - jnp.sum(member * first, axis=1, keepdims=True)
    pick_t[...] = one_hot(bucket == count((entries, rows), 1).astype(F32))
    pick[...] = one_hot(row_of(bucket, entries) == count((rows, entries), 0).astype(F32))
    lane = count((entries, LANES), 1) - (me * cap) % LANES
    inside = (lane >= 0) & (lane < cap)
    lane = lane.astype(F32)

    def list_slots(o, carry):
        hit = inside & (bucket - (o * cap).astype(F32) == lane)
        slots = jnp.sum(jnp.where(hit, slot, 0.0), axis=0, keepdims=True)
        slot_out[o] = jnp.broadcast_to(slots, (8, LANES))
        return carry

    lax.fori_loop(0, n, list_slots, 0)
    slot_in[me] = slot_out[me]

    pl.semaphore_wait(barrier, n)
    for c in range(PIECES):
        pair_copy(c).start()

    def slot_copy(o, source):
        return remote(slot_out.at[o], slot_in.at[source], slot_sem, o, source, at(o))

    others(lambda o: slot_copy(o, me).start())
    for c in range(PIECES):
        span = pl.ds(c * piece, piece)
        pair_copy(c).wait_recv()
        t = terms[freq, span, :] + other[span, :]
        high = t.astype(BF16)
        split[span, :LANES] = high
        split[span, LANES:] = (t - high.astype(F32)).astype(BF16)

    out[...] = dot(pick[...], split[...]).astype(BF16)

    def out_copy(o, source):
        return remote(out.at[place(o)], inn.at[place(source)], out_sem, o, source, at(o))

    others(lambda o: out_copy(o, me).start())
    inn[place(me), :] = out[place(me), :]

    others(lambda o: slot_copy(o, o).wait_recv())
    per = LANES // cap
    for g in range(rows // LANES):
        listed = slot_in[g * per, 0:1, :]
        for p in range(1, per):
            listed = listed + slot_in[g * per + p, 0:1, :]
        span = slice(g * LANES, (g + 1) * LANES)
        put[:, span] = one_hot(listed == count((blocks, LANES), 0).astype(F32))
        put_t[span, :] = one_hot(
            column_of(listed, LANES) == count((LANES, blocks), 1).astype(F32)
        )

    others(lambda o: out_copy(o, o).wait_recv())
    part = blocks // PIECES

    def total_copy(c):
        span = pl.ds(c * part, part)
        return remote(both.at[freq, span], both.at[freq, span], total_sem, c, c, partner)

    for c in range(PIECES):
        t = dot(put[c * part : (c + 1) * part, :], inn[...])
        both[freq, pl.ds(c * part, part), :] = t[:, :LANES] + t[:, LANES:]
        total_copy(c).start()
    small[-1].wait()
    for c in range(PIECES):
        span = pl.ds(c * part, part)
        total_copy(c).wait_recv()
        update = both[0, span, :] / (both[1, span, :] + damp[span, :])
        step[span, :] = update
        low[span, :] = update.astype(BF16)

    rep[...] = dot(put_t[...], low[...]).astype(BF16)

    def rep_copy(o, source):
        return remote(rep.at[place(o)], ret.at[place(source)], rep_sem, o, source, at(o))

    others(lambda o: rep_copy(o, me).start())
    ret[place(me), :] = rep[place(me), :]
    others(lambda o: rep_copy(o, o).wait_recv())
    entry[...] = dot(pick_t[...], ret[...])

    steps = len_ref.shape[1]

    def site_change(s, change):
        acc = jnp.zeros((freqs * comps, LANES), F32)
        for k in range(foot):
            e = s * foot + k
            acc = acc + jac[e].astype(F32) * entry[pl.ds(e, 1), :]
        total = jnp.sum(acc, axis=1, keepdims=True)
        return jnp.where(site_lane == s, total, change)

    change = lax.fori_loop(0, sites, site_change, jnp.zeros((freqs * comps, sites), F32), unroll=4)
    change_ref[...] = change.reshape(freqs, comps, sites)
    mine = jnp.zeros((freqs, LANES), F32)
    for a in range(steps):
        gap = residual - len_ref[0:1, a : a + 1] * change
        lost = (w_row * (gap * gap)).reshape(freqs, comps, sites)
        lost = jnp.sum(jnp.sum(lost, axis=1), axis=1, keepdims=True)
        mine = mine + jnp.where(count((freqs, LANES), 1) == a, lost, 0.0)
    curves[me] = jnp.zeros((8, LANES), F32)
    curves[me, :freqs, :] = mine

    def curve_copy(o, source):
        return remote(curves.at[me], curves.at[source], curve_sem, o, source, at(o))

    others(lambda o: curve_copy(o, me).start())
    others(lambda o: curve_copy(o, o).wait_recv())
    total = lax.fori_loop(
        0, n, lambda i, t: t + curves[i], jnp.zeros((8, LANES), F32)
    )
    curve_ref[...] = total[:freqs, :steps] * (1.0 / (n * sites * comps))

    for c in range(PIECES):
        pair_copy(c).wait_send()
        total_copy(c).wait_send()
    others(lambda o: slot_copy(o, me).wait_send())
    others(lambda o: out_copy(o, me).wait_send())
    others(lambda o: rep_copy(o, me).wait_send())
    others(lambda o: curve_copy(o, me).wait_send())


def store(*refs):
    count = len(refs) // 2
    sems = refs[-1]
    copies = [
        pltpu.make_async_copy(refs[i], refs[count + i], sems.at[i]) for i in range(count)
    ]
    for copy in copies:
        copy.start()
    for copy in copies:
        copy.wait()


def shards(jacobian, footprint, home, residual, weights, damping, step_lengths):
    sites, foot, freqs, comps, width = jacobian.shape
    blocks = damping.shape[0]
    groups = lax.axis_size("site")
    n = lax.axis_size("tile") * groups
    entries = sites * foot
    cap = 16
    while cap < 2 * entries // n:
        cap *= 2
    rows = n * cap
    sizes = (n, groups, cap, sites, foot, freqs, comps, blocks)
    hbm = pl.BlockSpec(memory_space=pltpu.HBM)
    free = pl.BlockSpec(memory_space=pl.ANY)
    vmem = pl.BlockSpec(memory_space=pltpu.VMEM)
    dma = pltpu.SemaphoreType.DMA
    results = pl.pallas_call(
        functools.partial(kernel, sizes),
        out_shape=(
            jax.ShapeDtypeStruct((blocks, width), F32),
            jax.ShapeDtypeStruct((freqs, comps, sites), F32),
            jax.ShapeDtypeStruct((freqs, step_lengths.shape[0]), F32),
        ),
        in_specs=[hbm] * 7,
        out_specs=(vmem,) * 3,
        scratch_shapes=[
            pltpu.VMEM((entries, freqs * comps, width), BF16),
            pltpu.VMEM((sites, foot), I32),
            pltpu.VMEM((home.shape[0] // LANES, LANES), I32),
            pltpu.VMEM((freqs, comps, sites), F32),
            pltpu.VMEM((1, sites), F32),
            pltpu.VMEM((1, step_lengths.shape[0]), F32),
            pltpu.VMEM((blocks, width), F32),
            pltpu.VMEM((2, entries, width), F32),
            pltpu.VMEM((entries, width), F32),
            pltpu.VMEM((entries, 2 * width), BF16),
            pltpu.VMEM((rows, entries), BF16),
            pltpu.VMEM((entries, rows), BF16),
            pltpu.VMEM((n, 8, LANES), F32),
            pltpu.VMEM((n, 8, LANES), F32),
            pltpu.VMEM((blocks, rows), BF16),
            pltpu.VMEM((rows, blocks), BF16),
            pltpu.VMEM((rows, 2 * width), BF16),
            pltpu.VMEM((rows, 2 * width), BF16),
            pltpu.VMEM((2, blocks, width), F32),
            pltpu.VMEM((blocks, width), BF16),
            pltpu.VMEM((rows, width), BF16),
            pltpu.VMEM((rows, width), BF16),
            pltpu.VMEM((entries, width), F32),
            pltpu.VMEM((n, 8, LANES), F32),
            dma((PIECES,)),
            dma((6,)),
            dma((2, PIECES)),
            dma((2, PIECES)),
            dma((2, n)),
            dma((2, n)),
            dma((2, n)),
            dma((2, n)),
        ],
        compiler_params=pltpu.CompilerParams(
            collective_id=0, has_side_effects=True, vmem_limit_bytes=VMEM_BYTES
        ),
    )(
        *(
            pltpu.with_memory_space_constraint(x, pltpu.HBM)
            for x in (
                jacobian.reshape(entries, freqs * comps, width),
                footprint,
                home.reshape(-1, LANES),
                residual.transpose(1, 2, 0),
                weights.reshape(1, -1),
                damping,
                step_lengths.reshape(1, -1),
            )
        )
    )
    model_step, change, curve = pl.pallas_call(
        store,
        out_shape=tuple(jax.ShapeDtypeStruct(r.shape, r.dtype) for r in results),
        in_specs=[free] * len(results),
        out_specs=(hbm,) * len(results),
        scratch_shapes=[dma((len(results),))],
        compiler_params=pltpu.CompilerParams(vmem_limit_bytes=VMEM_BYTES // 8),
    )(*results)
    return model_step, change.transpose(2, 0, 1), curve


def solution(mesh):
    placed = (
        P(("run", "tile", "site"), None, "freq", None, None),
        P(("run", "tile", "site"), None),
        P("run"),
        P(("run", "tile", "site"), "freq", None),
        P(("run", "tile", "site")),
        P(("run", "tile", "site"), None),
        P(),
    )
    return jax.shard_map(
        shards,
        mesh=mesh,
        in_specs=placed,
        out_specs=(
            P(("run", "tile", "site"), None),
            P(("run", "tile", "site"), "freq", None),
            P(("run", "freq"), None),
        ),
        check_vma=False,
    )
```
